32 devices in a mesh: dp: 4 (over z), seq: 8 (over y, x, core).
Axes of the slice: x: 2, y: 2, z: 4, core: 2. Of those that a mesh axis runs over, the one named last changes fastest.
Arguments:
- inputs: bfloat16 [16, 2048, 896], P('dp', 'seq'), may hold values from -6 to 6
- cotangent: bfloat16 [16, 2048, 896], P('dp', 'seq'), may hold values from -6 to 6
- segments: int32 [16, 2048], P('dp', 'seq'), may hold values from 0 to 10, as said below
- positions: int32 [16, 2048], P('dp', 'seq'), may hold values from 0 to 3998, as said below
- attn_master: float32 [1838080], P('seq')
- attn_moment: float32 [1838080], P('seq'), may hold values from -0.3 to 0.3
- attn_second: float32 [1838080], P('seq'), may hold values from 0.001 to 0.1
- ffn_master: float32 [13074432], P('seq')
- ffn_moment: float32 [13074432], P('seq'), may hold values from -0.3 to 0.3
- ffn_second: float32 [13074432], P('seq'), may hold values from 0.001 to 0.1
Outputs:
- result: bfloat16 [16, 2048, 896], P('dp', 'seq')
- grad_input: float32 [16, 2048, 896], P('dp', 'seq')
- attn_change: float32 [1838080], P('seq')
- moment_attn: float32 [1838080], P('seq')
- second_attn: float32 [1838080], P('seq')
- grad_attn: float32 [1838080], P('seq')
- ffn_change: float32 [13074432], P('seq')
- moment_ffn: float32 [13074432], P('seq')
- second_ffn: float32 [13074432], P('seq')
- grad_ffn: float32 [13074432], P('seq')
The draws below stay inside these ranges and needn't reach their ends.
Inputs may be any that keep to these rules, and one draw needn't show every extreme that they name: `segments`: in each sequence the document number starts at 0 and rises by one where a new document begins; every document has 200 to 2000 tokens, except the last of a sequence, which may be cut shorter. `positions`: A token's position is its index within its document plus an offset of 0 to 1999 drawn for each document.
All inputs are finite; a program needn't handle non-finite values.
Results may differ from the reference program's by a relative error of at most 0.025.
Values may be sent and summed in bfloat16 or wider, within the bound.
A program may use at most 640 MiB of HBM per device.

```python
import math
import jax
import jax.numpy as jnp
from jax import lax

D = 896
H = 14
KV = 2
HD = 64
FF = 4864
SEQ_LEN = 2048
DOC_MIN = 200
DOC_MAX = 2000
STEP = 8
B = 16
TOKENS = 32768
PA_PAD = 1838080
PF = 13074432


def document_layout(base_key):
    doc_slots = SEQ_LEN // DOC_MIN + 1
    length_key, offset_key = jax.random.split(base_key)
    doc_lengths = jax.random.randint(length_key, (B, doc_slots), DOC_MIN, DOC_MAX + 1, dtype=jnp.int32)
    doc_offsets = jax.random.randint(offset_key, (B, doc_slots), 0, DOC_MAX, dtype=jnp.int32)
    row_index = jnp.arange(B, dtype=jnp.int32)[:, None]
    slot_index = jnp.arange(doc_slots, dtype=jnp.int32)[None, :]
    first_row = row_index == 0
    last_row = (row_index == B - 1) & (slot_index == 0)
    doc_lengths = jnp.where(first_row, DOC_MIN, doc_lengths)
    doc_lengths = jnp.where(last_row, DOC_MAX, doc_lengths)
    doc_offsets = jnp.where(last_row, DOC_MAX - 1, doc_offsets)
    doc_ends = jnp.cumsum(doc_lengths, axis=1)
    doc_starts = doc_ends - doc_lengths
    places = jnp.arange(SEQ_LEN, dtype=jnp.int32)
    segment = jnp.sum((doc_ends[:, None, :] <= places[None, :, None]).astype(jnp.int32), axis=2)
    chosen = segment[:, :, None] == jnp.arange(doc_slots, dtype=jnp.int32)[None, None, :]
    opening = jnp.sum(jnp.where(chosen, doc_starts[:, None, :], 0), axis=2)
    offset = jnp.sum(jnp.where(chosen, doc_offsets[:, None, :], 0), axis=2)
    return (segment, places[None, :] - opening + offset)


def draw_segments(key, part):
    return document_layout(jax.random.fold_in(key, 17))[0]


def draw_positions(key, part):
    return document_layout(jax.random.fold_in(key, 17))[1]


def draw_attn_master(key, part):
    kv_width = KV * HD
    qkv_width = D + 2 * kv_width
    flat_index = jnp.arange(PA_PAD, dtype=jnp.int32)
    raw_noise = jax.random.normal(key, (PA_PAD,), jnp.float32)
    raw_noise = jnp.clip(raw_noise, -3.0, 3.0)
    gains_end = 2 * D
    bias_end = gains_end + qkv_width
    qkv_end = bias_end + D * qkv_width
    out_end = qkv_end + D * D
    spread_of = jnp.where(flat_index < gains_end, 0.15, jnp.where(flat_index < bias_end, 0.2, jnp.where(flat_index < qkv_end, D ** (-0.5), jnp.where(flat_index < out_end, 4.0 * D ** (-0.5), 0.02))))
    center = jnp.where(flat_index < gains_end, 1.0, 0.0)
    return center + spread_of * raw_noise


def draw_ffn_master(key, part):
    flat_index = jnp.arange(PF, dtype=jnp.int32)
    raw_noise = jax.random.normal(key, (PF,), jnp.float32)
    raw_noise = jnp.clip(raw_noise, -3.0, 3.0)
    spread_of = jnp.where(flat_index < 2 * D * FF, D ** (-0.5), FF ** (-0.5))
    return spread_of * raw_noise


def shard_levels(key, extent, cuts, low, top_value):
    def one(axis_at, shards_of):
        draws = jax.random.uniform(jax.random.fold_in(jax.random.fold_in(key, 6), axis_at), (shards_of,), jnp.float32, low / len(cuts), top_value / len(cuts))
        return jnp.repeat(jnp.exp(draws), extent[axis_at] // shards_of).reshape((-1,) + (1,) * (len(extent) - axis_at - 1))

    factor_of = one(*cuts[0])
    for cut in cuts[1:]:
        factor_of = factor_of * one(*cut)
    return factor_of


def scatter_about(key, shape, deviation, limit, shards=(), kind=jnp.bfloat16):
    entries = jax.random.normal(key, shape, jnp.float32) * deviation
    if len(shards) > 0:
        entries = shard_levels(key, shape, shards, -0.22, 0.18) * entries
    return jnp.clip(entries, min=-limit, max=limit).astype(kind)


def setup_inputs(seed: int = 0) -> dict:
    seeds = jax.random.split(jax.random.key(seed), 11)
    inputs = scatter_about(seeds[0], (B, SEQ_LEN, D), 1.0, 6.0, ((0, 4), (1, 8)))
    cotangent = scatter_about(seeds[1], (B, SEQ_LEN, D), 1.0, 6.0, ((0, 4), (1, 8)))
    segments = draw_segments(jax.random.fold_in(seeds[10], 71), 0)
    positions = draw_positions(jax.random.fold_in(seeds[10], 71), 0)
    attn_master = draw_attn_master(jax.random.fold_in(seeds[10], 71), 0)
    attn_moment = scatter_about(seeds[5], (PA_PAD,), 0.05, 0.3, ((0, 8),), jnp.float32)
    attn_second = jnp.clip(jnp.exp(math.log(0.1) - 4.6051702 * jax.random.uniform(seeds[6], (PA_PAD,), jnp.float32) ** shard_levels(seeds[6], (PA_PAD,), ((0, 8),), -0.2, 0.2)), 0.001, 0.1)
    ffn_master = draw_ffn_master(jax.random.fold_in(seeds[10], 71), 0)
    ffn_moment = scatter_about(seeds[8], (PF,), 0.05, 0.3, ((0, 8),), jnp.float32)
    ffn_second = jnp.clip(jnp.exp(math.log(0.1) - 4.6051702 * jax.random.uniform(seeds[9], (PF,), jnp.float32) ** shard_levels(seeds[9], (PF,), ((0, 8),), -0.2, 0.2)), 0.001, 0.1)
    return dict(inputs=inputs, cotangent=cotangent, segments=segments, positions=positions, attn_master=attn_master, attn_moment=attn_moment, attn_second=attn_second, ffn_master=ffn_master, ffn_moment=ffn_moment, ffn_second=ffn_second)


@jax.custom_vjp
def low(v):
    return lax.optimization_barrier(v.astype(jnp.bfloat16)).astype(jnp.float32)

@jax.custom_vjp
def low_back(v):
    return v

def low_keep(v):
    return (low(v), None)

def low_pass(kept, grad):
    return (grad,)

def back_keep(v):
    return (v, None)

def back_low(kept, grad):
    return (low(grad),)
low.defvjp(low_keep, low_pass)
low_back.defvjp(back_keep, back_low)
norm_eps = 1e-06
rope_base = 1000000.0
first_decay = 0.9
second_decay = 0.95
learn_rate = 0.01
weight_decay = 0.1
adam_eps = 1e-08
masked_score = -1e+30
highest = lax.Precision.HIGHEST

def split_weights(attn_flat, ffn_flat):
    kv_width = KV * HD
    qkv_width = D + 2 * kv_width
    offset = 2 * D + qkv_width
    gain_one = attn_flat[0:D].astype(jnp.float32)
    gain_two = attn_flat[D:2 * D].astype(jnp.float32)
    bias_qkv = attn_flat[2 * D:offset].astype(jnp.float32)
    w_qkv = attn_flat[offset:offset + D * qkv_width].reshape(D, qkv_width)
    w_out = attn_flat[offset + D * qkv_width:offset + D * qkv_width + D * D].reshape(D, D)
    w_gu = ffn_flat[:2 * D * FF].reshape(D, 2 * FF)
    w_down = ffn_flat[2 * D * FF:].reshape(FF, D)
    return (gain_one, gain_two, bias_qkv, w_qkv, w_out, w_gu, w_down)

def rope_tables(pos_values):
    halfway = HD // 2
    frequency = jnp.exp(jnp.arange(halfway, dtype=jnp.float32) * (-2.0 * math.log(rope_base) / HD))
    angles = pos_values.astype(jnp.float32)[..., None] * frequency
    return (jnp.cos(angles), jnp.sin(angles))

def rotate(values, cosine, sine_table):
    halfway = values.shape[-1] // 2
    front_half = values[..., :halfway]
    back_half = values[..., halfway:]
    return jnp.concatenate([front_half * cosine - back_half * sine_table, back_half * cosine + front_half * sine_table], axis=-1)

def forward_one(x_row, attn_flat, ffn_flat, seg_row, pos_row):
    gain_one, gain_two, bias_qkv, w_qkv, w_out, w_gu, w_down = split_weights(attn_flat, ffn_flat)
    kv_width = KV * HD
    groups = H // KV
    inv_one = lax.rsqrt(lax.optimization_barrier(jnp.mean(x_row * x_row, axis=-1, keepdims=True)) + norm_eps)
    normed_one = low(x_row * inv_one * gain_one)
    qkv_proj = low_back(jnp.dot(normed_one, w_qkv, precision=highest) + bias_qkv)
    cosine, sine_table = rope_tables(pos_row)
    cos_heads = cosine[:, None, :]
    sin_heads = sine_table[:, None, :]
    queries = low(rotate(qkv_proj[:, :D].reshape(-1, H, HD), cos_heads, sin_heads))
    key_rows = low(rotate(qkv_proj[:, D:D + kv_width].reshape(-1, KV, HD), cos_heads, sin_heads))
    value_rows = low(qkv_proj[:, D + kv_width:].reshape(-1, KV, HD))
    grouped = queries.reshape(-1, KV, groups, HD)
    raw_scores = jnp.einsum('qkgd,skd->kgqs', grouped, key_rows, precision=highest)
    scores = low_back(raw_scores * HD ** (-0.5))
    places = jnp.arange(x_row.shape[0], dtype=jnp.int32)
    allowed = (seg_row[:, None] == seg_row[None, :]) & (places[:, None] >= places[None, :])
    masked = jnp.where(allowed, scores, masked_score)
    log_total = jax.nn.logsumexp(masked, axis=-1, keepdims=True)
    soft_prob = low(jnp.exp(masked - log_total))
    mixed_heads = jnp.einsum('kgqs,skd->qkgd', soft_prob, value_rows, precision=highest).reshape(-1, D)
    mixed_heads = low(low_back(mixed_heads))
    branch = low_back(jnp.dot(mixed_heads, w_out, precision=highest))
    residual = x_row + branch
    inv_two = lax.rsqrt(lax.optimization_barrier(jnp.mean(residual * residual, axis=-1, keepdims=True)) + norm_eps)
    normed_two = low(residual * inv_two * gain_two)
    gate_up = low_back(jnp.dot(normed_two, w_gu, precision=highest))
    gate_part = gate_up[:, :FF]
    up_part = gate_up[:, FF:]
    hidden = low(jax.nn.silu(gate_part) * up_part)
    return residual + low_back(jnp.dot(hidden, w_down, precision=highest))

def adam_step(master, moment, second, gradient):
    moment_new = first_decay * moment + (1.0 - first_decay) * gradient
    second_new = second_decay * second + (1.0 - second_decay) * gradient * gradient
    corrected = moment_new / (1.0 - first_decay ** STEP)
    spread_root = jnp.sqrt(second_new / (1.0 - second_decay ** STEP))
    change = -learn_rate * (corrected / (spread_root + adam_eps) + weight_decay * master)
    return (change, moment_new, second_new)

def reference(inputs, cotangent, segments, positions, attn_master, attn_moment, attn_second, ffn_master, ffn_moment, ffn_second):
    attn_flat = low(attn_master)
    ffn_flat = low(ffn_master)

    def per_seq(totals, row_data):
        x_row, cot_row, seg_row, pos_row = row_data

        def forward(row_in, attn_in, ffn_in):
            return forward_one(row_in, attn_in, ffn_in, seg_row, pos_row)
        y_row, pullback = jax.vjp(forward, x_row.astype(jnp.float32), attn_flat, ffn_flat)
        grad_row, grad_a, grad_f = pullback(cot_row.astype(jnp.float32))
        return ((totals[0] + grad_a, totals[1] + grad_f), (y_row.astype(jnp.bfloat16), grad_row))
    initial = (jnp.zeros(attn_master.shape, jnp.float32), jnp.zeros(ffn_master.shape, jnp.float32))
    sums_out, rows_out = lax.scan(per_seq, initial, (inputs, cotangent, segments, positions))
    token_scale = 1.0 / math.sqrt(TOKENS)
    grad_attn = sums_out[0] * token_scale
    grad_ffn = sums_out[1] * token_scale
    attn_change, moment_attn, second_attn = adam_step(attn_master, attn_moment, attn_second, grad_attn)
    ffn_change, moment_ffn, second_ffn = adam_step(ffn_master, ffn_moment, ffn_second, grad_ffn)
    return (rows_out[0], rows_out[1], attn_change, moment_attn, second_attn, grad_attn, ffn_change, moment_ffn, second_ffn, grad_ffn)
```

```python
import functools
import math

import jax
import jax.numpy as jnp
from jax import lax
from jax.experimental import pallas as pl
from jax.experimental.pallas import tpu as pltpu
from jax.sharding import PartitionSpec as P

D = 896
H = 14
KV = 2
GROUP = H // KV
HD = 64
FF = 4864
STEP = 8
QKV = D + 2 * KV * HD
F32 = jnp.float32
BF = jnp.bfloat16

norm_eps = 1e-06
rope_base = 1000000.0
first_decay = 0.9
second_decay = 0.95
learn_rate = 0.01
weight_decay = 0.1
adam_eps = 1e-08
masked_score = -1e30
MIB = 1 << 20

PIECE = 4256
PIECE_TILES = 532
GU_PIECES = 16
COLS = 2 * FF // 128
STEPS = FF // 256
GAIN_ROWS = (2 * D + QKV) // 128
OUT_ROW = GAIN_ROWS + D * QKV // 128
USED_ROWS = OUT_ROW + D * D // 128


def nn(a, b):
    return lax.dot_general(a, b, (((1,), (0,)), ((), ())), preferred_element_type=F32)


def nt(a, b):
    return lax.dot_general(a, b, (((1,), (1,)), ((), ())), preferred_element_type=F32)


def params(mib):
    return pltpu.CompilerParams(vmem_limit_bytes=mib * MIB)


def adam_step(master, moment, second, gradient):
    moment_new = first_decay * moment + (1.0 - first_decay) * gradient
    second_new = second_decay * second + (1.0 - second_decay) * gradient * gradient
    corrected = moment_new / (1.0 - first_decay**STEP)
    spread_root = jnp.sqrt(second_new / (1.0 - second_decay**STEP))
    change = -learn_rate * (corrected / (spread_root + adam_eps) + weight_decay * master)
    return (change, moment_new, second_new)


def pack_kernel(kind_ref, x_ref, o_ref):
    kind = kind_ref[pl.program_id(0)]

    @pl.when(kind == 0)
    def _():
        def body(c, _):
            for r in range(7):
                o_ref[c * 7 + r] = x_ref[pl.ds(r * 608 + c, 8, stride=COLS), :].astype(BF)
            return 0

        lax.fori_loop(0, COLS, body, 0, unroll=4)

    @pl.when(kind == 1)
    def _():
        def body(r, _):
            for c in range(7):
                o_ref[r * 7 + c] = x_ref[pl.ds(r * 56 + c, 8, stride=7), :].astype(BF)
            return 0

        lax.fori_loop(0, 76, body, 0, unroll=4)


def pack(kinds, flat):
    count = flat.shape[0] // PIECE
    return pl.pallas_call(
        pack_kernel,
        out_shape=jax.ShapeDtypeStruct((count * PIECE_TILES, 8, 128), BF),
        grid_spec=pltpu.PrefetchScalarGridSpec(
            num_scalar_prefetch=1,
            grid=(count,),
            in_specs=[pl.BlockSpec((PIECE, 128), lambda i, k: (i, 0))],
            out_specs=pl.BlockSpec((PIECE_TILES, 8, 128), lambda i, k: (i, 0, 0)),
        ),
        compiler_params=params(32),
        name="pack_ffn",
    )(kinds, flat)


def adam_kernel(kind_ref, g_ref, w_ref, m_ref, v_ref, ch_ref, mo_ref, se_ref, gr_ref):
    kind = kind_ref[pl.program_id(0)]

    @pl.when(kind == 0)
    def _():
        def body(c, _):
            for r in range(7):
                gr_ref[pl.ds(r * 608 + c, 8, stride=COLS), :] = g_ref[c * 7 + r].astype(F32)
            return 0

        lax.fori_loop(0, COLS, body, 0, unroll=4)

    @pl.when(kind == 1)
    def _():
        def body(r, _):
            for c in range(7):
                gr_ref[pl.ds(r * 56 + c, 8, stride=7), :] = g_ref[r * 7 + c].astype(F32)
            return 0

        lax.fori_loop(0, 76, body, 0, unroll=4)

    def update(i, _):
        rows = pl.ds(pl.multiple_of(i * 56, 8), 56)
        change, moment, second = adam_step(
            w_ref[rows, :], m_ref[rows, :], v_ref[rows, :], gr_ref[rows, :]
        )
        ch_ref[rows, :] = change
        mo_ref[rows, :] = moment
        se_ref[rows, :] = second
        return 0

    lax.fori_loop(0, PIECE // 56, update, 0)


def adam_tiles(kinds, tiles, master, moment, second):
    count = master.shape[0] // PIECE
    flat = pl.BlockSpec((PIECE, 128), lambda i, k: (i, 0))
    return pl.pallas_call(
        adam_kernel,
        out_shape=(jax.ShapeDtypeStruct(master.shape, F32),) * 4,
        grid_spec=pltpu.PrefetchScalarGridSpec(
            num_scalar_prefetch=1,
            grid=(count,),
            in_specs=[pl.BlockSpec((PIECE_TILES, 8, 128), lambda i, k: (i, 0, 0)), flat, flat, flat],
            out_specs=(flat,) * 4,
        ),
        compiler_params=params(48),
        name="adam_ffn",
    )(kinds, tiles, master, moment, second)


def tiles_of_flat(flat):
    cut = 2 * D * FF
    gu = flat[:cut].reshape(GU_PIECES, 7, 8, COLS, 128).transpose(0, 3, 1, 2, 4)
    down = flat[cut:].reshape(FF // 8, 8, 7, 128).transpose(0, 2, 1, 3)
    return jnp.concatenate([gu.reshape(-1, 8, 128), down.reshape(-1, 8, 128)])


def flat_of_tiles(tiles):
    cut = GU_PIECES * PIECE_TILES
    gu = tiles[:cut].reshape(GU_PIECES, COLS, 7, 8, 128).transpose(0, 2, 3, 1, 4)
    down = tiles[cut:].reshape(FF // 8, 7, 8, 128).transpose(0, 2, 1, 3)
    return jnp.concatenate([gu.reshape(-1), down.reshape(-1)])


def qkv_kernel(
    x_ref, flat_ref, cos_ref, sin_ref,
    qt_ref, kv_ref, nt_ref, wqkv_ref, wout_ref, gains_ref,
    wide, bias_s,
):
    tokens = x_ref.shape[0]
    span = kv_ref.shape[1]
    rows = flat_ref.shape[0]
    chunk = rows // 4
    chunk -= chunk % 16
    for i in range(4):
        lo, hi = i * chunk, (i + 1) * chunk if i < 3 else rows
        wide[lo:hi, :] = flat_ref[lo:hi, :].astype(F32)
    for c in range(7):
        lanes = slice(c * 128, (c + 1) * 128)
        gains_ref[0:1, lanes] = wide[c : c + 1, :]
        gains_ref[1:2, lanes] = wide[7 + c : 8 + c, :]
    for c in range(9):
        bias_s[0:1, c * 128 : (c + 1) * 128] = wide[14 + c : 15 + c, :]

    def unpack(r, _):
        out_rows = pl.ds(pl.multiple_of(r * 16, 16), 16)
        for c in range(9):
            wqkv_ref[out_rows, c * 128 : (c + 1) * 128] = wide[
                pl.ds(GAIN_ROWS + r * 144 + c, 16, stride=9), :
            ].astype(BF)
        for c in range(7):
            wout_ref[out_rows, c * 128 : (c + 1) * 128] = wide[
                pl.ds(OUT_ROW + r * 112 + c, 16, stride=7), :
            ].astype(BF)
        return 0

    lax.fori_loop(0, D // 16, unpack, 0, unroll=2)
    gain = gains_ref[0:1, :]
    for i in range(tokens // span):
        sl = slice(i * span, (i + 1) * span)
        x = x_ref[sl, :].astype(F32)
        inv = lax.rsqrt(jnp.mean(x * x, axis=1, keepdims=True) + norm_eps)
        normed = (x * inv * gain).astype(BF)
        nt_ref[:, sl] = normed.T
        proj = nn(normed, wqkv_ref[...]) + bias_s[...]
        cos, sin = cos_ref[:, sl], sin_ref[:, sl]
        turned = proj[:, : D + KV * HD].T
        for h in range(H + KV):
            a = turned[h * HD : h * HD + HD // 2, :]
            b = turned[h * HD + HD // 2 : (h + 1) * HD, :]
            front, back = a * cos - b * sin, b * cos + a * sin
            if h < H:
                qt_ref[h * HD : h * HD + HD // 2, sl] = (front.astype(BF) * 0.125).astype(BF)
                qt_ref[h * HD + HD // 2 : (h + 1) * HD, sl] = (back.astype(BF) * 0.125).astype(BF)
            else:
                k = h - H
                both = jnp.concatenate([front, back], axis=0).astype(BF)
                kv_ref[i, :, k * HD : (k + 1) * HD] = both.T
        kv_ref[i, :, KV * HD :] = proj[:, D + KV * HD :].astype(BF)


def qkv_forward(x, flat, cos, sin, count):
    tokens = x.shape[0]
    return pl.pallas_call(
        qkv_kernel,
        out_shape=(
            jax.ShapeDtypeStruct((D, tokens), BF),
            jax.ShapeDtypeStruct((count, tokens // count, 2 * KV * HD), BF),
            jax.ShapeDtypeStruct((D, tokens), BF),
            jax.ShapeDtypeStruct((D, QKV), BF),
            jax.ShapeDtypeStruct((D, D), BF),
            jax.ShapeDtypeStruct((2, D), F32),
        ),
        scratch_shapes=[pltpu.VMEM(flat.shape, F32), pltpu.VMEM((1, QKV), F32)],
        compiler_params=params(56),
        name="qkv_forward",
    )(x, flat, cos, sin)


def tail_kernel(
    scale, dq_ref, dkv_ref, x_ref, nt_ref, wqkv_ref, gains_ref, cos_ref, sin_ref, gres_ref, dwout_ref, ggain_ref,
    gin_ref, flat_ref, wide, gt_s, g_s,
):
    tokens = x_ref.shape[0]
    span = dkv_ref.shape[1]
    gt_s[0:D, :] = dq_ref[...]
    for i in range(tokens // span):
        sl = slice(i * span, (i + 1) * span)
        cos, sin = cos_ref[:, sl], sin_ref[:, sl]
        both = dkv_ref[i].T
        for k in range(KV):
            a = both[k * HD : k * HD + HD // 2, :].astype(F32)
            b = both[k * HD + HD // 2 : (k + 1) * HD, :].astype(F32)
            base = D + k * HD
            gt_s[base : base + HD // 2, sl] = (a * cos + b * sin).astype(BF)
            gt_s[base + HD // 2 : base + HD, sl] = (b * cos - a * sin).astype(BF)
        gt_s[D + KV * HD :, sl] = both[KV * HD :, :]
    gain = gains_ref[0:1, :]
    grad_gain = jnp.zeros((1, D), F32)
    grad_bias = jnp.zeros((1, QKV), F32)
    for i in range(tokens // span):
        sl = slice(i * span, (i + 1) * span)
        g = gt_s[:, sl].T
        g_s[sl, :] = g
        grad_bias += jnp.sum(g.astype(F32), axis=0, keepdims=True)
        gn = nt(g, wqkv_ref[...])
        x = x_ref[sl, :].astype(F32)
        inv = lax.rsqrt(jnp.mean(x * x, axis=1, keepdims=True) + norm_eps)
        grad_gain += jnp.sum(gn * (x * inv), axis=0, keepdims=True)
        weighted = gn * gain
        mean = jnp.mean(x * weighted, axis=1, keepdims=True)
        gin_ref[sl, :] = gres_ref[sl, :] + inv * weighted - x * (inv * inv * inv * mean)
    grad_gain *= scale
    grad_bias *= scale
    for c in range(7):
        lanes = slice(c * 128, (c + 1) * 128)
        wide[c : c + 1, :] = grad_gain[:, lanes]
        wide[7 + c : 8 + c, :] = ggain_ref[:, lanes]
    for c in range(9):
        wide[14 + c : 15 + c, :] = grad_bias[:, c * 128 : (c + 1) * 128]
    for q in range(0, D, 128):
        dw = nn(nt_ref[q : q + 128, :], g_s[...]) * scale
        for r in range(8):
            row = q + r * 16
            for c in range(9):
                wide[pl.ds(GAIN_ROWS + row * 9 + c, 16, stride=9), :] = dw[
                    r * 16 : (r + 1) * 16, c * 128 : (c + 1) * 128
                ]

    def pack_out(r, _):
        rows = pl.ds(pl.multiple_of(r * 16, 16), 16)
        for c in range(7):
            wide[pl.ds(OUT_ROW + r * 112 + c, 16, stride=7), :] = dwout_ref[
                rows, c * 128 : (c + 1) * 128
            ].astype(F32)
        return 0

    lax.fori_loop(0, D // 16, pack_out, 0, unroll=2)
    rows = flat_ref.shape[0]
    wide[USED_ROWS:rows, :] = jnp.zeros((rows - USED_ROWS, 128), F32)
    chunk = rows // 4
    chunk -= chunk % 16
    for i in range(4):
        lo, hi = i * chunk, (i + 1) * chunk if i < 3 else rows
        flat_ref[lo:hi, :] = wide[lo:hi, :].astype(BF)


def tail_backward(scale, rows, dq, dkv, x, normed_t, wqkv, gains, cos, sin, gres, dwout, ggain):
    tokens = x.shape[0]
    return pl.pallas_call(
        functools.partial(tail_kernel, scale),
        out_shape=(
            jax.ShapeDtypeStruct((tokens, D), F32),
            jax.ShapeDtypeStruct((rows, 128), BF),
        ),
        scratch_shapes=[
            pltpu.VMEM((rows, 128), F32),
            pltpu.VMEM((QKV, tokens), BF),
            pltpu.VMEM((tokens, QKV), BF),
        ],
        compiler_params=params(58),
        name="tail_backward",
    )(dq, dkv, x, normed_t, wqkv, gains, cos, sin, gres, dwout, ggain)


def bias_of(kb,st_ref,L,rank):
    rows=lax.broadcasted_iota(jnp.int32,(L,L),0)+kb*L
    qp=lax.broadcasted_iota(jnp.int32,(L,L),1)+rank*L
    return jnp.where((rows>=st_ref[0])&(rows<=qp),0.0,masked_score).astype(F32)
def fwd_kernel(lo_ref, qt_ref, kv_ref, st_ref, mix_ref, mixt_ref, lse_ref, m_s, l_s, o_s, bias_s):
    s=pl.program_id(0); L=qt_ref.shape[1]
    lo=lo_ref[s]; rank=lo_ref[4]
    m_s[...]=jnp.full_like(m_s, masked_score); l_s[...]=jnp.zeros_like(l_s); o_s[...]=jnp.zeros_like(o_s)
    def body(kb,_):
        bias_s[...]=bias_of(kb,st_ref,L,rank)
        kvb=kv_ref[kb,0]
        vt=kvb[:,128:].T
        for g in range(2):
            k=kvb[:,g*64:(g+1)*64]
            v=vt[g*64:(g+1)*64]
            for h in range(g*GROUP,(g+1)*GROUP):
                sl=slice(h*64,(h+1)*64)
                sc=nn(k,qt_ref[sl,:])+bias_s[...]
                mo=m_s[h:h+1,:]
                mn=jnp.maximum(mo,jnp.max(sc,axis=0,keepdims=True))
                p=jnp.exp(sc-mn)
                al=jnp.exp(mo-mn)
                m_s[h:h+1,:]=mn
                l_s[h:h+1,:]=l_s[h:h+1,:]*al+jnp.sum(p,axis=0,keepdims=True)
                o_s[sl,:]=o_s[sl,:]*al+nn(v,p.astype(BF))
        return 0
    lax.fori_loop(lo,rank+1,body,0)
    lse_ref[...]=(m_s[...]+jnp.log(l_s[...]))[None]
    for h in range(H):
        sl=slice(h*64,(h+1)*64)
        mixt_ref[sl,:]=(o_s[sl,:]*(1.0/l_s[h:h+1,:])).astype(BF)
    mix_ref[...]=mixt_ref[...].T
def attn_fwd(lo,qt,kv,starts):
    n=kv.shape[0]; nb=kv.shape[1]; L=kv.shape[2]; T=qt.shape[1]
    return pl.pallas_call(fwd_kernel,
      out_shape=(jax.ShapeDtypeStruct((T,D),BF),jax.ShapeDtypeStruct((D,T),BF),jax.ShapeDtypeStruct((nb,H,L),F32)),
      grid_spec=pltpu.PrefetchScalarGridSpec(num_scalar_prefetch=1,grid=(nb,),
       in_specs=[pl.BlockSpec((D,L),lambda s,a:(0,s)),pl.BlockSpec((n,1,L,256),lambda s,a:(0,s,0,0)),pl.BlockSpec((1,1,L),lambda s,a:(s,0,0))],
       out_specs=(pl.BlockSpec((L,D),lambda s,a:(s,0)),pl.BlockSpec((D,L),lambda s,a:(0,s)),pl.BlockSpec((1,H,L),lambda s,a:(s,0,0))),
       scratch_shapes=[pltpu.VMEM((H,L),F32),pltpu.VMEM((H,L),F32),pltpu.VMEM((D,L),F32),pltpu.VMEM((L,L),F32)]),
      compiler_params=pltpu.CompilerParams(vmem_limit_bytes=40<<20))(lo,qt,kv,starts)
def bwd_kernel(lo_ref, qt_ref, dot_ref, mixt_ref, kv_ref, st_ref, lse_ref, cos_ref, sin_ref, dq_ref, dkv_ref, dl_s, dq_s, bias_s, p_s, ds_s, qs_s, dos_s):
    s=pl.program_id(0); L=qt_ref.shape[1]
    lo=lo_ref[s]; rank=lo_ref[4]
    dkv_ref[...]=jnp.zeros_like(dkv_ref)
    dq_s[...]=jnp.zeros_like(dq_s)
    for h in range(H):
        sl=slice(h*64,(h+1)*64); g,hh=divmod(h,GROUP)
        dl_s[h:h+1,:]=jnp.sum(dot_ref[sl,:].astype(F32)*mixt_ref[sl,:].astype(F32),axis=0,keepdims=True)
        qs_s[g,:,hh*L:(hh+1)*L]=qt_ref[sl,:]
        dos_s[g,:,hh*L:(hh+1)*L]=dot_ref[sl,:]
    def body(kb,_):
        bias_s[...]=bias_of(kb,st_ref,L,rank)
        kvb=kv_ref[kb,0]
        kt=kvb[:,:128].T
        for g in range(2):
            k=kvb[:,g*64:(g+1)*64]
            v=kvb[:,128+g*64:128+(g+1)*64]
            for h in range(g*GROUP,(g+1)*GROUP):
                hh=h-g*GROUP
                sl=slice(h*64,(h+1)*64)
                sc=nn(k,qt_ref[sl,:])+bias_s[...]
                p=jnp.exp(sc-lse_ref[0,h:h+1,:])
                p_s[:,hh*L:(hh+1)*L]=p.astype(BF)
                dp=nn(v,dot_ref[sl,:])
                ds=(p*(dp-dl_s[h:h+1,:])).astype(BF)
                ds_s[:,hh*L:(hh+1)*L]=ds
                dq_s[sl,:]+=nn(kt[g*64:(g+1)*64],ds)
            dk=nt(ds_s[...],qs_s[g])
            dv=nt(p_s[...],dos_s[g])
            dkv_ref[kb,0,:,g*64:(g+1)*64]=dk.astype(BF)
            dkv_ref[kb,0,:,128+g*64:128+(g+1)*64]=dv.astype(BF)
        return 0
    lax.fori_loop(lo,rank+1,body,0)
    c=cos_ref[...]*0.125; sn=sin_ref[...]*0.125
    for h in range(H):
        a=dq_s[h*64:h*64+32,:]; b=dq_s[h*64+32:(h+1)*64,:]
        dq_ref[h*64:h*64+32,:]=(a*c+b*sn).astype(BF)
        dq_ref[h*64+32:(h+1)*64,:]=(b*c-a*sn).astype(BF)
def attn_bwd(lo,qt,dot,mixt,kv,starts,lse,cos,sin):
    n=kv.shape[0]; nb=kv.shape[1]; L=kv.shape[2]; T=qt.shape[1]
    col=lambda r: pl.BlockSpec((r,L),lambda s,a:(0,s))
    return pl.pallas_call(bwd_kernel,
      out_shape=(jax.ShapeDtypeStruct((D,T),BF),jax.ShapeDtypeStruct((n,nb,L,256),BF)),
      grid_spec=pltpu.PrefetchScalarGridSpec(num_scalar_prefetch=1,grid=(nb,),
       in_specs=[col(D),col(D),col(D),pl.BlockSpec((n,1,L,256),lambda s,a:(0,s,0,0)),pl.BlockSpec((1,1,L),lambda s,a:(s,0,0)),pl.BlockSpec((1,H,L),lambda s,a:(s,0,0)),col(32),col(32)],
       out_specs=(col(D),pl.BlockSpec((n,1,L,256),lambda s,a:(0,s,0,0))),
       scratch_shapes=[pltpu.VMEM((H,L),F32),pltpu.VMEM((D,L),F32),pltpu.VMEM((L,L),F32),pltpu.VMEM((L,GROUP*L),BF),pltpu.VMEM((L,GROUP*L),BF),pltpu.VMEM((2,64,GROUP*L),BF),pltpu.VMEM((2,64,GROUP*L),BF)]),
      compiler_params=pltpu.CompilerParams(vmem_limit_bytes=40<<20))(lo,qt,dot,mixt,kv,starts,lse,cos,sin)


def mid_kernel(scale, x_hbm, ct_hbm, mixed_hbm, mixedt_hbm, wout_hbm, gain_ref, wg_ref, wu_ref, wd_ref,
   res_out, gres_out, gmix_out, dwout_out, ggain_out, dw_out,
   c_s, ct_s, n_s, nt_s, resid, acc_o, acc_n, wgu, wdn, hid, ggu, tmp, tmpw, dwbuf, ddbuf, sems, osem, dsem):
    j=pl.program_id(0); nsteps=pl.num_programs(0)
    T=c_s.shape[0]; CH=256 if T%256==0 else T; NCH=T//CH
    slot=lax.rem(j,2)
    def cp(src,dst,k): return pltpu.make_async_copy(src,dst,sems.at[k])
    def gcopies(s,jj):
        out=[]
        for half in range(2):
            for t in range(16):
                out.append(pltpu.make_async_copy(dwbuf.at[s,half,t], dw_out.at[pl.ds(t*76+half*38+2*jj,2)], osem.at[s]))
        out.append(pltpu.make_async_copy(ddbuf.at[s], dw_out.at[pl.ds(1216+32*jj,32)], dsem.at[s]))
        return out
    @pl.when(j==0)
    def _():
        a=cp(ct_hbm,c_s,0); a.start()
        b=cp(mixed_hbm,tmp,1); b.start()
        c=cp(wout_hbm,tmpw,2); c.start()
        d=cp(x_hbm,n_s,3); d.start()
        a.wait();
        for i in range(NCH):
            ct_s[:,i*CH:(i+1)*CH]=c_s[i*CH:(i+1)*CH,:].T
        b.wait(); c.wait(); d.wait()
        for i in range(NCH):
            sl=slice(i*CH,(i+1)*CH)
            r=n_s[sl,:].astype(F32)+nn(tmp[sl,:],tmpw[...])
            resid[sl,:]=r
            inv=lax.rsqrt(jnp.mean(r*r,axis=1,keepdims=True)+norm_eps)
            nv=(r*inv*gain_ref[1:2,:]).astype(BF)
            n_s[sl,:]=nv
            nt_s[:,sl]=nv.T
            acc_o[sl,:]=r
        acc_n[...]=jnp.zeros_like(acc_n)
    @pl.when(j>=2)
    def _():
        for c in gcopies(slot,j-2): c.wait()
    for c in range(2):
        wgu[:,c*128:(c+1)*128]=wg_ref[:,c].reshape(D,128)
        wgu[:,256+c*128:256+(c+1)*128]=wu_ref[:,c].reshape(D,128)
    for c in range(7):
        wdn[:,c*128:(c+1)*128]=wd_ref[:,c].reshape(256,128)
    for i in range(NCH):
        sl=slice(i*CH,(i+1)*CH)
        gu=nn(n_s[sl,:],wgu[...])
        g=gu[:,:256]; u=gu[:,256:]
        gh=nt(c_s[sl,:],wdn[...])
        s=1.0/(1.0+jnp.exp(-g))
        silu=g*s
        h=(silu*u).astype(BF)
        ghs=gh*s
        gg=(ghs*u*(1.0+(g-silu))).astype(BF)
        gu_=(ghs*g).astype(BF)
        hid[sl,:]=h
        ggu[sl,:256]=gg
        ggu[sl,256:]=gu_
        acc_o[sl,:]+=nn(h,wdn[...])
        acc_n[sl,:]+=nt(ggu[sl,:],wgu[...])
    for q in range(0,D,128):
        d=nn(nt_s[q:q+128,:],ggu[...])*scale
        db=d.astype(BF)
        for r in range(16):
            row=q//8+r; t=row//7; w=row%7
            for half in range(2):
                for c in range(2):
                    dwbuf[slot,half,t,c,w]=db[r*8:(r+1)*8,half*256+c*128:half*256+(c+1)*128]
        e=(nn(ct_s[q:q+128,:],hid[...])*scale).astype(BF)
        et=e.T
        ddbuf[slot,:,q//128]=et.reshape(32,8,128)
    for c in gcopies(slot,j): c.start()
    @pl.when(j==nsteps-1)
    def _():
        w=cp(wout_hbm,tmpw,2); w.start()
        b=cp(mixedt_hbm,nt_s,1); b.start()
        w.wait()
        for i in range(NCH):
            sl=slice(i*CH,(i+1)*CH)
            n_s[sl,:]=acc_o[sl,:].astype(BF)
            r=resid[sl,:]; gn=acc_n[sl,:]
            inv=lax.rsqrt(jnp.mean(r*r,axis=1,keepdims=True)+norm_eps)
            ri=r*inv
            gg=jnp.sum(gn*ri,axis=0,keepdims=True)*scale
            if i==0: ggain_out[...]=gg
            else: ggain_out[...]+=gg
            wt=gn*gain_ref[1:2,:]
            m=jnp.mean(r*wt,axis=1,keepdims=True)
            gr=c_s[sl,:].astype(F32)+inv*wt-r*(inv*inv*inv*m)
            acc_n[sl,:]=gr
            gb=gr.astype(BF)
            c_s[sl,:]=gb
            ct_s[:,sl]=nt(tmpw[...],gb).astype(BF)
        o1=cp(n_s,res_out,0); o1.start()
        o2=cp(acc_n,gres_out,3); o2.start()
        o3=cp(ct_s,gmix_out,2); o3.start()
        b.wait()
        for q in range(0,D,128):
            dwout_out[q:q+128,:]=(nn(nt_s[q:q+128,:],c_s[...])*scale).astype(BF)
        o1.wait();o2.wait();o3.wait()
        for c in gcopies(1-slot,j-1): c.wait()
        for c in gcopies(slot,j): c.wait()
def mid(scale,x,ct,mixed,mixedt,wout,gain,wt):
    T=x.shape[0]
    any_=pl.BlockSpec(memory_space=pl.ANY)
    return pl.pallas_call(functools.partial(mid_kernel,scale),
      out_shape=(jax.ShapeDtypeStruct((T,D),BF),jax.ShapeDtypeStruct((T,D),F32),jax.ShapeDtypeStruct((D,T),BF),
        jax.ShapeDtypeStruct((D,D),BF),jax.ShapeDtypeStruct((1,D),F32),jax.ShapeDtypeStruct((1824,7,8,128),BF)),
      grid=(STEPS,),
      in_specs=[any_,any_,any_,any_,any_,pl.BlockSpec((2,D),lambda j:(0,0)),
        pl.BlockSpec((16,2,7,8,128),lambda j:(0,j,0,0,0)),
        pl.BlockSpec((16,2,7,8,128),lambda j:(0,STEPS+j,0,0,0)),
        pl.BlockSpec((32,7,8,128),lambda j:(38+j,0,0,0))],
      out_specs=(any_,any_,any_,pl.BlockSpec((D,D),lambda j:(0,0)),pl.BlockSpec((1,D),lambda j:(0,0)),any_),
      scratch_shapes=[pltpu.VMEM((T,D),BF),pltpu.VMEM((D,T),BF),pltpu.VMEM((T,D),BF),pltpu.VMEM((D,T),BF),
        pltpu.VMEM((T,D),F32),pltpu.VMEM((T,D),F32),pltpu.VMEM((T,D),F32),
        pltpu.VMEM((D,512),BF),pltpu.VMEM((256,D),BF),pltpu.VMEM((T,256),BF),pltpu.VMEM((T,512),BF),
        pltpu.VMEM((T,D),BF),pltpu.VMEM((D,D),BF),
        pltpu.VMEM((2,2,16,2,7,8,128),BF),pltpu.VMEM((2,32,7,8,128),BF),
        pltpu.SemaphoreType.DMA((4,)),pltpu.SemaphoreType.DMA((2,)),pltpu.SemaphoreType.DMA((2,))],
      compiler_params=pltpu.CompilerParams(vmem_limit_bytes=60<<20))(x,ct,mixed,mixedt,wout,gain,wt.reshape(24,76,7,8,128),wt.reshape(24,76,7,8,128),wt.reshape(1824,7,8,128))


def per_device(
    inputs,
    cotangent,
    segments,
    positions,
    attn_master,
    attn_moment,
    attn_second,
    ffn_master,
    ffn_moment,
    ffn_second,
):
    count, span = inputs.shape[0], inputs.shape[1]
    parts = lax.axis_size("seq")
    rank = lax.axis_index("seq")
    tokens = count * span
    scale = 1.0 / math.sqrt(tokens * parts * lax.axis_size("dp"))
    aligned = ffn_master.shape[0] % (PIECE * 128) == 0
    attn_flat = lax.all_gather(attn_master.reshape(-1, 128).astype(BF), "seq", axis=0, tiled=True)
    seg_all = lax.all_gather(segments, "seq", axis=0, tiled=False)
    if aligned:
        pieces = ffn_master.shape[0] // (PIECE * 128)
        kinds = (rank * pieces + jnp.arange(pieces, dtype=jnp.int32) >= GU_PIECES).astype(jnp.int32)
        mine = pack(kinds, ffn_master.reshape(-1, 128))
        tiles = lax.all_gather(mine, "seq", axis=0, tiled=True)
    else:
        tiles = tiles_of_flat(lax.all_gather(ffn_master.astype(BF), "seq", axis=0, tiled=True))
    x = inputs.reshape(tokens, D)
    frequency = jnp.exp(jnp.arange(HD // 2, dtype=F32) * (-2.0 * math.log(rope_base) / HD))
    angles = frequency[:, None] * positions.reshape(1, tokens).astype(F32)
    cos, sin = jnp.cos(angles), jnp.sin(angles)
    qt, kv, normed_t, wqkv, wout, gains = qkv_forward(x, attn_flat, cos, sin, count)
    kv_all = lax.all_gather(kv, "seq", axis=0, tiled=False)
    starts = jnp.sum(
        (seg_all.transpose(1, 0, 2).reshape(count, 1, parts * span) < segments[:, :, None]).astype(jnp.int32),
        axis=2,
    )
    bounds = jnp.concatenate([starts[:, 0] // span, rank[None].astype(jnp.int32)])
    starts = starts[:, None, :]
    mixed, mixed_t, log_total = attn_fwd(bounds, qt, kv_all, starts)
    result, grad_res, grad_mixed_t, dwout, ggain, dtiles = mid(
        scale, x, cotangent.reshape(tokens, D), mixed, mixed_t, wout, gains, tiles
    )
    dtiles = dtiles.reshape(tiles.shape)
    if aligned:
        owned = lax.psum_scatter(dtiles, "seq", scatter_dimension=0, tiled=True)
    else:
        owned = lax.psum_scatter(flat_of_tiles(dtiles), "seq", scatter_dimension=0, tiled=True)
    owned = lax.psum(owned, "dp")
    dq, dkv = attn_bwd(bounds, qt, grad_mixed_t, mixed_t, kv_all, starts, log_total, cos, sin)
    dkv = lax.psum_scatter(dkv, "seq", scatter_dimension=0, tiled=False)
    grad_input, dattn = tail_backward(
        scale, attn_flat.shape[0], dq, dkv, x, normed_t, wqkv, gains, cos, sin, grad_res, dwout, ggain
    )
    grad_attn = lax.psum_scatter(dattn, "seq", scatter_dimension=0, tiled=True)
    grad_attn, owned = lax.optimization_barrier((grad_attn, owned))
    grad_attn = lax.psum(grad_attn, "dp").astype(F32).reshape(attn_master.shape)
    attn_change, moment_attn, second_attn = adam_step(
        attn_master, attn_moment, attn_second, grad_attn
    )
    if aligned:
        ffn_change, moment_ffn, second_ffn, grad_ffn = (
            v.reshape(ffn_master.shape)
            for v in adam_tiles(
                kinds, owned, *(v.reshape(-1, 128) for v in (ffn_master, ffn_moment, ffn_second))
            )
        )
    else:
        grad_ffn = owned.astype(F32)
        ffn_change, moment_ffn, second_ffn = adam_step(ffn_master, ffn_moment, ffn_second, grad_ffn)
    return (
        result.reshape(inputs.shape),
        grad_input.reshape(inputs.shape),
        attn_change,
        moment_attn,
        second_attn,
        grad_attn,
        ffn_change,
        moment_ffn,
        second_ffn,
        grad_ffn,
    )


def solution(mesh):
    rows, flat = P("dp", "seq", None), P("seq")
    return jax.shard_map(
        per_device,
        mesh=mesh,
        in_specs=(rows, rows, P("dp", "seq"), P("dp", "seq")) + (flat,) * 6,
        out_specs=(rows, rows) + (flat,) * 8,
        check_vma=False,
    )
```
